256 devices in a mesh: seq: 64 (over y, z, core), head: 4 (over x).
Axes of the slice: x: 4, y: 4, z: 8, core: 2. Of those that a mesh axis runs over, the one named last changes fastest.
Arguments:
- queries: bfloat16 [49152, 2560], P('seq', 'head'), may hold values from -12 to 12
- keys: bfloat16 [49152, 2560], P('seq', 'head'), may hold values from -6 to 6
- values: bfloat16 [49152, 2560], P('seq', 'head'), may hold values from -6 to 6
- w_out: bfloat16 [2560, 5120], P('head'), may hold values from -0.125 to 0.125
- selected: int32 [768, 16], P('seq'), may hold values from 0 to 767, as said below
- home: int32 [768], replicated, may hold values from 0 to 767, as said below
Outputs:
- projected: bfloat16 [49152, 5120], P('seq', 'head')
The draws below stay inside these ranges and needn't reach their ends.
Inputs may be any that keep to these rules, and one draw needn't show every extreme that they name: `selected`: every row names 16 different cubes. Taken together, the rows of the 12 slots of one index of seq name at most 1 different cubes whose slots lie on any one index of seq, and exactly 1 for some index. `home`: A permutation: every slot holds exactly one cube; slot j lies on index j // 12 of seq.
All inputs are finite; a program needn't handle non-finite values.
Results may differ from the reference program's by a relative error of at most 0.0057.
Values may be sent and summed in bfloat16 or wider, within the bound.
No kernel may reach another device: no remote copies, remote signals or barrier semaphores. Data moves between devices by JAX's collectives and lax.ppermute only.
A program may use at most 192 MiB of HBM per device.

```python
import jax
import jax.numpy as jnp
from jax import lax

D = 5120
HEADS = 20
HEAD_DIM = 128
CUBE = 64
SEL = 16
CUBES_DEV = 12
CAP = 1
NCUBES = 768
TOKENS = 49152
HF = 2560


def plan_tables(key):
    base_key = jax.random.fold_in(key, 1000)
    key_perm, key_local, key_shift, key_pick = jax.random.split(base_key, 4)
    device_count = NCUBES // CUBES_DEV
    pool_size = device_count * CAP
    order_scores = jax.random.randint(key_perm, (NCUBES,), 0, NCUBES, dtype=jnp.int32) * NCUBES + jnp.arange(NCUBES, dtype=jnp.int32)
    home_table = jnp.argsort(order_scores).astype(jnp.int32)
    cube_at = jnp.argsort(home_table).astype(jnp.int32)
    local_scores = jax.random.randint(key_local, (device_count, device_count, CUBES_DEV), 0, CUBES_DEV, dtype=jnp.int32) * CUBES_DEV + jnp.arange(CUBES_DEV, dtype=jnp.int32)
    local_pick = jnp.argsort(local_scores, axis=-1)[:, :, :CAP].astype(jnp.int32)
    shifts = jax.random.randint(key_shift, (device_count,), 0, device_count, dtype=jnp.int32)
    owner_order = (jnp.arange(device_count, dtype=jnp.int32)[None, :] + shifts[:, None]) % device_count
    local_order = jnp.take_along_axis(local_pick, owner_order[:, :, None], axis=1)
    pool_slots = (owner_order[:, :, None] * CUBES_DEV + local_order).reshape(device_count, pool_size)
    counter = jnp.arange(pool_size, dtype=jnp.int32)
    random_part = jax.random.randint(key_pick, (device_count, CUBES_DEV, pool_size), 0, pool_size, dtype=jnp.int32)
    pick_scores = (random_part + 1) * pool_size + counter[None, None, :]
    leading = (jnp.arange(CUBES_DEV, dtype=jnp.int32) == 0)[None, :, None]
    pick_scores = jnp.where(leading, counter[None, None, :], pick_scores)
    chosen = jnp.argsort(pick_scores, axis=-1)[:, :, :SEL].astype(jnp.int32)
    spread_pool = jnp.broadcast_to(pool_slots[:, None, :], (device_count, CUBES_DEV, pool_size))
    slot_lists = jnp.take_along_axis(spread_pool, chosen, axis=-1).reshape(NCUBES, SEL)
    selected_table = cube_at[slot_lists].astype(jnp.int32)
    return (home_table, selected_table)


def key_field(key):
    field_key = jax.random.fold_in(key, 2000)
    key_normal = jax.random.fold_in(field_key, 0)
    normal_part = jnp.clip(1.5 * jax.random.normal(key_normal, (TOKENS, HF), jnp.float32), -6.0, 6.0)
    blended = normal_part
    cubes = blended.reshape(NCUBES, CUBE, HF)
    second = cubes[:, 1, :]
    cubes = cubes.at[:, 1, :].set(second)
    return cubes.reshape(TOKENS, HF)


def draw_selected(key, part):
    home_table, selected_table = plan_tables(key)
    return selected_table


def draw_home(key, part):
    home_table, selected_table = plan_tables(key)
    return home_table


def draw_keys(key, part):
    return key_field(key).astype(jnp.bfloat16)


def draw_queries(key, part):
    key = jax.random.fold_in(key, 5)
    key_normal = jax.random.fold_in(key, 0)
    normal_part = jnp.clip(1.5 * jax.random.normal(key_normal, (TOKENS, HF), jnp.float32), -6.0, 6.0)
    cubes = normal_part.reshape(NCUBES, CUBE, HF)
    first_row = cubes[:, 0, :]
    cubes = cubes.at[:, 0, :].set(first_row)
    return cubes.reshape(TOKENS, HF).astype(jnp.bfloat16)


def level_of(stream_key, extent, shards, low, top_value):
    loudness, own = 1.0, jax.random.fold_in(stream_key, 6)
    for axis_at, parts in shards:
        draws = jnp.exp(jax.random.uniform(jax.random.fold_in(own, axis_at), (parts,), jnp.float32, low / len(shards), top_value / len(shards)))
        loudness = loudness * jnp.repeat(draws, extent[axis_at] // parts).reshape([-1 if axis == axis_at else 1 for axis in range(len(extent))])
    return loudness


def bell_draw(rng, dims, width, reach, cuts=(), held_as=jnp.bfloat16):
    result = width * jax.random.normal(rng, dims, jnp.float32)
    if cuts:
        result = result * level_of(rng, dims, cuts, -0.22, 0.18)
    return jnp.clip(result, -reach, reach).astype(held_as)


def setup_inputs(seed: int = 0) -> dict:
    key_of = jax.random.split(jax.random.key(seed), 7)
    return {
        "queries": draw_queries(jax.random.fold_in(key_of[6], 71), 0),
        "keys": draw_keys(jax.random.fold_in(key_of[6], 71), 0),
        "values": bell_draw(key_of[2], (TOKENS, HF), 1.0, 6.0, ((0, 64), (1, 4))),
        "w_out": bell_draw(key_of[3], (HF, D), HF ** -0.5, 0.125, ((0, 4),)),
        "selected": draw_selected(jax.random.fold_in(key_of[6], 71), 0),
        "home": draw_home(jax.random.fold_in(key_of[6], 71), 0),
    }


def reference(queries, keys, values, w_out, selected, home):
    query_blocks = queries.reshape(NCUBES, CUBE, HEADS, HEAD_DIM)
    key_blocks = keys.reshape(NCUBES, CUBE, HEADS, HEAD_DIM)
    value_blocks = values.reshape(NCUBES, CUBE, HEADS, HEAD_DIM)
    slot_lists = home[selected].astype(jnp.int32)

    def attend(item):
        block, slot_row = item
        near_keys = key_blocks[slot_row].reshape(SEL * CUBE, HEADS, HEAD_DIM).astype(jnp.float32)
        near_values = value_blocks[slot_row].reshape(SEL * CUBE, HEADS, HEAD_DIM).astype(jnp.float32)
        scores = jnp.einsum("qhd,khd->hqk", block.astype(jnp.float32), near_keys) * (HEAD_DIM ** -0.5)
        peak = jnp.max(scores, axis=2, keepdims=True)
        raised = jnp.exp(scores - peak)
        probs = (raised / jnp.sum(raised, axis=2, keepdims=True)).astype(jnp.bfloat16)
        mixed = jnp.einsum("hqk,khd->qhd", probs.astype(jnp.float32), near_values)
        return mixed.astype(jnp.bfloat16)

    attended = lax.map(attend, (query_blocks, slot_lists)).reshape(TOKENS, HEADS * HEAD_DIM)
    return jnp.dot(attended, w_out, preferred_element_type=jnp.float32).astype(jnp.bfloat16)
```

```python
import functools

import jax
import jax.numpy as jnp
from jax import lax
from jax.experimental import pallas as pl
from jax.experimental.pallas import tpu as pltpu
from jax.sharding import Mesh
from jax.sharding import PartitionSpec as P

HEAD_DIM = 128
CUBE = 64
SEL = 16
NY, NZ, NC = 4, 8, 2
NPLANE = NY * NC


def shift(n, d):
    return [(i, (i + d) % n) for i in range(n)]


def rows_of(at):
    return pl.ds(pl.multiple_of(at * CUBE, CUBE), CUBE)


def pick_kernel(want_ref, from_z_ref, *refs):
    sources, out = refs[:-1], refs[-1]
    width = 2 * HEAD_DIM
    for head, source in enumerate(sources):
        lanes = pl.ds(head * width, width)

        def step(at, carry, source=source, lanes=lanes):
            owner = at % NZ
            out[rows_of(at), lanes] = source[rows_of(from_z_ref[owner] + want_ref[at]), :]
            return carry

        lax.fori_loop(0, NPLANE * NZ, step, 0, unroll=8)


def pick(want, from_z, gathered, first, heads):
    width = 2 * HEAD_DIM
    rows = gathered.shape[0]
    out = jax.ShapeDtypeStruct((NPLANE * NZ * CUBE, heads * width), jnp.bfloat16)
    return pl.pallas_call(
        pick_kernel,
        out_shape=out,
        grid_spec=pltpu.PrefetchScalarGridSpec(
            num_scalar_prefetch=2,
            grid=(1,),
            in_specs=[
                pl.BlockSpec((rows, width), lambda i, *_, at=at: (0, at))
                for at in range(first, first + heads)
            ],
            out_specs=pl.BlockSpec(out.shape, lambda i, *_: (0, 0)),
        ),
        cost_estimate=pl.CostEstimate(flops=0, bytes_accessed=4 * out.size, transcendentals=0),
        compiler_params=pltpu.CompilerParams(vmem_limit_bytes=40 << 20),
        name="pick",
    )(want, from_z, *[gathered] * heads)


def attend_kernel(place_ref, q_ref, *refs, cubes, per):
    arrived, (o_ref, ks, vs) = refs[:-3], refs[-3:]
    for head, kv_ref in enumerate(arrived):
        lanes = pl.ds(head * HEAD_DIM, HEAD_DIM)

        def step(group, carry, kv_ref=kv_ref, lanes=lanes):
            for u in range(per):
                for t in range(SEL):
                    rows = rows_of(place_ref[(group * per + u) * SEL + t])
                    ks[u, t * CUBE : (t + 1) * CUBE, :] = kv_ref[rows, :HEAD_DIM]
                    vs[u, t * CUBE : (t + 1) * CUBE, :] = kv_ref[rows, HEAD_DIM:]
            for u in range(per):
                rows = rows_of(group * per + u)
                scores = lax.dot_general(
                    q_ref[rows, lanes],
                    ks[u],
                    (((1,), (1,)), ((), ())),
                    preferred_element_type=jnp.float32,
                ) * (HEAD_DIM**-0.5)
                peak = jnp.max(scores, axis=1, keepdims=True)
                raised = jnp.exp(scores - peak)
                total = jnp.sum(raised, axis=1, keepdims=True)
                probs = (raised * (1.0 / total)).astype(jnp.bfloat16)
                mixed = jnp.dot(probs, vs[u], preferred_element_type=jnp.float32)
                o_ref[rows, lanes] = mixed.astype(jnp.bfloat16)
            return carry

        lax.fori_loop(0, cubes // per, step, 0)


def attend(places, queries, arrived, first):
    tokens, width = queries.shape[0], len(arrived) * HEAD_DIM
    cubes = tokens // CUBE
    per = next(p for p in (4, 3, 2, 1) if cubes % p == 0)
    return pl.pallas_call(
        functools.partial(attend_kernel, cubes=cubes, per=per),
        out_shape=jax.ShapeDtypeStruct((tokens, width), jnp.bfloat16),
        grid_spec=pltpu.PrefetchScalarGridSpec(
            num_scalar_prefetch=1,
            grid=(1,),
            in_specs=[pl.BlockSpec((tokens, width), lambda i, _: (0, first // len(arrived)))]
            + [
                pl.BlockSpec((a.shape[0], 2 * HEAD_DIM), lambda i, _, at=at: (0, at))
                for a, at in arrived
            ],
            out_specs=pl.BlockSpec((tokens, width), lambda i, _: (0, 0)),
            scratch_shapes=[pltpu.VMEM((per, SEL * CUBE, HEAD_DIM), jnp.bfloat16)] * 2,
        ),
        cost_estimate=pl.CostEstimate(
            flops=4 * tokens * SEL * CUBE * width,
            bytes_accessed=4 * NPLANE * NZ * CUBE * width,
            transcendentals=tokens * SEL * CUBE * len(arrived),
        ),
        compiler_params=pltpu.CompilerParams(vmem_limit_bytes=24 << 20),
        name="attend",
    )(places, queries, *(a for a, _ in arrived))


def project_kernel(*refs, parts, first):
    rows, weights = refs[:parts], refs[parts : 2 * parts]
    total = None if first else refs[2 * parts][...]
    for a, w in zip(rows, weights):
        term = jnp.dot(a[...], w[...], preferred_element_type=jnp.float32)
        total = term if total is None else total + term
    refs[-1][...] = total.astype(refs[-1].dtype)


def project(terms, weights, before, out_type):
    rows = [a for group, _ in terms for a in group]
    parts = len(rows)
    tokens, columns = rows[0].shape[0], weights[0].shape[1]
    tile = 256
    in_specs = [pl.BlockSpec(a.shape, lambda n: (0, 0)) for a in rows]
    in_specs += [
        pl.BlockSpec((a.shape[1], tile), lambda n, at=head * HEAD_DIM // a.shape[1]: (at, n))
        for group, head in terms
        for a in group
    ]
    block = pl.BlockSpec((tokens, tile), lambda n: (0, n))
    extra = [] if before is None else [before]
    return pl.pallas_call(
        functools.partial(project_kernel, parts=parts, first=before is None),
        out_shape=jax.ShapeDtypeStruct((tokens, columns), out_type),
        grid=(columns // tile,),
        in_specs=in_specs + [block] * len(extra),
        out_specs=block,
        cost_estimate=pl.CostEstimate(
            flops=2 * sum(a.size for a in rows) * columns,
            bytes_accessed=8 * tokens * columns,
            transcendentals=0,
        ),
        compiler_params=pltpu.CompilerParams(vmem_limit_bytes=24 << 20),
        name="project",
    )(*rows, *weights * len(terms), *extra)


def after(arrays, earlier):
    held = lax.optimization_barrier(tuple(arrays) + tuple(earlier))
    return held[: len(arrays)]


def per_device(queries, keys, values, w_out, selected, home):
    tokens, width = queries.shape
    cubes_here = tokens // CUBE
    heads_here = width // HEAD_DIM
    groups = lax.axis_size("head")
    y, z, core = (lax.axis_index(a) for a in ("y", "z", "core"))
    me = lax.axis_index("head")

    def columns(a, h):
        return a[:, h * HEAD_DIM : (h + 1) * HEAD_DIM]

    def pack(heads):
        pieces = [columns(a, h) for h in heads for a in (keys, values)]
        return jnp.concatenate(pieces, axis=1)

    catalog = jnp.arange(home.shape[0], dtype=jnp.int32)
    slot_of = jnp.sum(
        jnp.where(selected[:, :, None] == catalog[None, None, :], home[None, None, :], 0), axis=2
    ).reshape(-1)
    owner = slot_of // cubes_here
    places = (owner // (NZ * NC) * NC + owner % NC) * NZ + (z - owner // NC % NZ) % NZ

    every_slot = lax.all_gather(slot_of, ("y", "core"), axis=0)
    owners = every_slot // cubes_here
    mine = (owners // (NZ * NC) == y) & (owners % NC == core)
    step = (z - owners // NC % NZ) % NZ
    matches = mine[:, None, :] & (step[:, None, :] == jnp.arange(NZ, dtype=jnp.int32)[:, None])
    want = jnp.max(jnp.where(matches, every_slot[:, None, :] % cubes_here, 0), axis=2)
    want = want.reshape(-1)
    from_z = (z - jnp.arange(NZ, dtype=jnp.int32)) % NZ * cubes_here

    w_columns = width_out = w_out.shape[1] // groups
    weights = []
    for d in range(groups):
        part = lax.dynamic_slice_in_dim(w_out, (me + d) % groups * w_columns, width_out, axis=1)
        weights.append(lax.ppermute(part, "head", shift(groups, d)) if d else part)

    def exchange(outgoing):
        return lax.all_to_all(outgoing, ("y", "core"), split_axis=0, concat_axis=0, tiled=True)

    def spread(rows):
        return [rows] + [lax.ppermute(rows, "head", shift(groups, d)) for d in range(1, groups)]

    def gather(heads, earlier=()):
        (chunk,) = after((pack(heads),), earlier)
        return lax.all_gather(chunk, "z", axis=0).reshape(NZ * tokens, -1)

    g01 = gather((0, 1))
    g23 = gather((2, 3))
    g4 = gather((4,), (g01,))

    g01, want, _, _ = after((g01, want, weights[1], weights[3]), ())
    in01 = exchange(pick(want, from_z, g01, 0, 2))
    in01, _ = after((in01, weights[2]), ())
    rows01 = attend(places, queries, [(in01, 0), (in01, 1)], 0)

    g23, rows01 = after((g23, rows01), ())
    out2, out3 = pick(want, from_z, g23, 0, 1), pick(want, from_z, g23, 1, 1)
    in2 = exchange(out2)
    rows01, out3 = after((rows01, out3), (out2,))
    all01 = after(spread(rows01), ())

    in2, g4, out3 = after((in2, g4, out3), all01[1:])
    in3 = exchange(out3)
    out4 = pick(want, from_z, g4, 0, 1)
    total = project([(after(all01, (out3,)), 0)], weights, None, jnp.float32)
    rows2 = attend(places, queries, [(in2, 0)], 2)

    in3, out4, rows2 = after((in3, out4, rows2), (total,))
    in4 = exchange(out4)
    rows3 = attend(places, queries, [(in3, 0)], 3)
    all2, all3 = spread(rows2), spread(rows3)
    (in4,) = after((in4,), (rows3,))
    rows4 = attend(places, queries, [(in4, 0)], 4)
    terms = [(all2, 2), (all3, 3), (spread(rows4), 4)]
    return project(terms, weights, total, jnp.bfloat16)


def solution(mesh):
    fine = Mesh(
        mesh.devices.reshape(NY, NZ, NC, mesh.shape["head"]), ("y", "z", "core", "head")
    )
    seq = ("y", "z", "core")
    in_specs = (
        P(seq, "head"),
        P(seq, "head"),
        P(seq, "head"),
        P("head", None),
        P(seq, None),
        P(),
    )
    return jax.shard_map(
        per_device, mesh=fine, in_specs=in_specs, out_specs=P(seq, "head"), check_vma=False
    )
```

```python
import functools

import jax
import jax.numpy as jnp
from jax import lax
from jax.experimental import pallas as pl
from jax.experimental.pallas import tpu as pltpu
from jax.sharding import Mesh
from jax.sharding import PartitionSpec as P

HEAD_DIM = 128
CUBE = 64
SEL = 16
NY, NZ, NC = 4, 8, 2
NPLANE = NY * NC
LOG2_E = 1.4426950408889634


def shift(n, d):
    return [(i, (i + d) % n) for i in range(n)]


def rows_of(at):
    return pl.ds(pl.multiple_of(at * CUBE, CUBE), CUBE)


def pick_kernel(cube_ref, *refs, blocks):
    sources, out = refs[:-1], refs[-1]
    width = 2 * HEAD_DIM
    for head, source in enumerate(sources):
        lanes = pl.ds(head * width, width)

        def step(at, carry, source=source, lanes=lanes):
            out[rows_of(at), lanes] = source[rows_of(cube_ref[at]), :]
            return carry

        lax.fori_loop(0, blocks, step, 0, unroll=8)


def pick(cubes, source, first, heads):
    width = 2 * HEAD_DIM
    rows, blocks = source.shape[0], cubes.shape[0]
    out = jax.ShapeDtypeStruct((blocks * CUBE, heads * width), jnp.bfloat16)
    return pl.pallas_call(
        functools.partial(pick_kernel, blocks=blocks),
        out_shape=out,
        grid_spec=pltpu.PrefetchScalarGridSpec(
            num_scalar_prefetch=1,
            grid=(1,),
            in_specs=[
                pl.BlockSpec((rows, width), lambda i, *_, at=at: (0, at))
                for at in range(first, first + heads)
            ],
            out_specs=pl.BlockSpec(out.shape, lambda i, *_: (0, 0)),
        ),
        cost_estimate=pl.CostEstimate(flops=0, bytes_accessed=4 * out.size, transcendentals=0),
        compiler_params=pltpu.CompilerParams(vmem_limit_bytes=40 << 20),
        name="pick",
    )(cubes, *[source] * heads)


def attend_kernel(place_ref, *refs, cubes, per):
    heads = (len(refs) - 3) // 2
    asking, arrived, (o_ref, ks, vs) = refs[:heads], refs[heads:-3], refs[-3:]
    for head in range(heads):
        lanes = pl.ds(head * HEAD_DIM, HEAD_DIM)

        def step(group, carry, q_ref=asking[head], kv_ref=arrived[head], lanes=lanes):
            for u in range(per):
                for t in range(SEL):
                    rows = rows_of(place_ref[(group * per + u) * SEL + t])
                    ks[u, t * CUBE : (t + 1) * CUBE, :] = kv_ref[rows, :HEAD_DIM]
                    vs[u, t * CUBE : (t + 1) * CUBE, :] = kv_ref[rows, HEAD_DIM:]
            for u in range(per):
                rows = rows_of(group * per + u)
                scores = lax.dot_general(
                    q_ref[rows, :],
                    ks[u],
                    (((1,), (1,)), ((), ())),
                    preferred_element_type=jnp.float32,
                )
                peak = jnp.max(scores, axis=1, keepdims=True)
                raised = jnp.exp2((scores - peak) * (HEAD_DIM**-0.5 * LOG2_E))
                total = jnp.sum(raised, axis=1, keepdims=True)
                probs = (raised * (1.0 / total)).astype(jnp.bfloat16)
                mixed = jnp.dot(probs, vs[u], preferred_element_type=jnp.float32)
                o_ref[rows, lanes] = mixed.astype(jnp.bfloat16)
            return carry

        lax.fori_loop(0, cubes // per, step, 0)


def attend(places, queries, arrived, first):
    tokens, width = queries.shape[0], len(arrived) * HEAD_DIM
    cubes = tokens // CUBE
    per = next(p for p in (4, 3, 2, 1) if cubes % p == 0)
    return pl.pallas_call(
        functools.partial(attend_kernel, cubes=cubes, per=per),
        out_shape=jax.ShapeDtypeStruct((tokens, width), jnp.bfloat16),
        grid_spec=pltpu.PrefetchScalarGridSpec(
            num_scalar_prefetch=1,
            grid=(1,),
            in_specs=[
                pl.BlockSpec((tokens, HEAD_DIM), lambda i, _, head=head: (0, head))
                for head in range(first, first + len(arrived))
            ]
            + [
                pl.BlockSpec((a.shape[0], 2 * HEAD_DIM), lambda i, _, at=at: (0, at))
                for a, at in arrived
            ],
            out_specs=pl.BlockSpec((tokens, width), lambda i, _: (0, 0)),
            scratch_shapes=[pltpu.VMEM((per, SEL * CUBE, HEAD_DIM), jnp.bfloat16)] * 2,
        ),
        cost_estimate=pl.CostEstimate(
            flops=4 * tokens * SEL * CUBE * width,
            bytes_accessed=4 * NPLANE * NZ * CUBE * width,
            transcendentals=tokens * SEL * CUBE * len(arrived),
        ),
        compiler_params=pltpu.CompilerParams(vmem_limit_bytes=24 << 20),
        name="attend",
    )(places, *[queries] * len(arrived), *(a for a, _ in arrived))


def project_kernel(*refs, terms, heads):
    rows, weights, before = refs[:terms], refs[terms : terms + heads], refs[terms + heads : -2]
    out, beside = refs[-2:]

    @pl.when(pl.program_id(0) == 0)
    def _():
        at = 0
        for a in rows:
            beside[:, at : at + a.shape[1]] = a[...]
            at += a.shape[1]

    below = jnp.concatenate([w[...] for w in weights], axis=0)
    total = jnp.dot(beside[...], below, preferred_element_type=jnp.float32)
    for earlier in before:
        total = total + earlier[...]
    out[...] = total.astype(out.dtype)


def project(terms, weights, before, out_type):
    rows = [a for group, _ in terms for a in group]
    tokens, columns = rows[0].shape[0], weights[0].shape[1]
    tile = 256
    block = pl.BlockSpec((tokens, tile), lambda n: (0, n))
    in_specs = [pl.BlockSpec(a.shape, lambda n: (0, 0)) for a in rows]
    below = []
    for group, first in terms:
        for a, w in zip(group, weights):
            for head in range(first, first + a.shape[1] // HEAD_DIM):
                in_specs.append(pl.BlockSpec((HEAD_DIM, tile), lambda n, head=head: (head, n)))
                below.append(w)
    extra = [] if before is None else [before]
    width = sum(a.shape[1] for a in rows)
    return pl.pallas_call(
        functools.partial(project_kernel, terms=len(rows), heads=len(below)),
        out_shape=jax.ShapeDtypeStruct((tokens, columns), out_type),
        grid=(columns // tile,),
        in_specs=in_specs + [block] * len(extra),
        out_specs=block,
        scratch_shapes=[pltpu.VMEM((tokens, width), jnp.bfloat16)],
        cost_estimate=pl.CostEstimate(
            flops=2 * tokens * width * columns,
            bytes_accessed=2 * (tokens * width + width * columns + tokens * columns),
            transcendentals=0,
        ),
        compiler_params=pltpu.CompilerParams(vmem_limit_bytes=40 << 20),
        name="project",
    )(*rows, *below, *extra)


def after(arrays, earlier):
    held = lax.optimization_barrier(tuple(arrays) + tuple(earlier))
    return held[: len(arrays)]


def per_device(queries, keys, values, w_out, selected, home):
    tokens, width = queries.shape
    cubes_here = tokens // CUBE
    heads_here = width // HEAD_DIM
    groups = lax.axis_size("head")
    y, z, core = (lax.axis_index(a) for a in ("y", "z", "core"))
    me = lax.axis_index("head")

    def columns(a, h):
        return a[:, h * HEAD_DIM : (h + 1) * HEAD_DIM]

    def exchange(outgoing):
        return lax.all_to_all(outgoing, ("y", "core"), split_axis=0, concat_axis=0, tiled=True)

    def pack(heads):
        pieces = [columns(a, h) for h in heads for a in (keys, values)]
        return jnp.concatenate(pieces, axis=1)

    catalog = jnp.arange(home.shape[0], dtype=jnp.int32)
    slot_of = jnp.sum(
        jnp.where(selected[:, :, None] == catalog[None, None, :], home[None, None, :], 0), axis=2
    ).reshape(-1)
    owner = slot_of // cubes_here
    places = (owner // (NZ * NC) * NC + owner % NC) * NZ + (z - owner // NC % NZ) % NZ

    plane = lax.all_gather(slot_of, ("y", "core"), axis=0)
    owners = plane // cubes_here
    mine = (owners // (NZ * NC) == y) & (owners % NC == core)
    step = (z - owners // NC % NZ) % NZ
    steps = jnp.arange(NZ, dtype=jnp.int32)[:, None]
    matches = mine[:, None, :] & (step[:, None, :] == steps)
    want = jnp.max(jnp.where(matches, plane[:, None, :] % cubes_here, 0), axis=2)
    from_z = (z - steps[:, 0]) % NZ * cubes_here
    want = (want + from_z).reshape(-1)

    w_columns = width_out = w_out.shape[1] // groups
    weights = []
    for d in range(groups):
        part = lax.dynamic_slice_in_dim(w_out, (me + d) % groups * w_columns, width_out, axis=1)
        weights.append(lax.ppermute(part, "head", shift(groups, d)) if d else part)

    def spread(rows):
        return [rows] + [lax.ppermute(rows, "head", shift(groups, d)) for d in range(1, groups)]

    def gather(heads, earlier=()):
        (chunk,) = after((pack(heads),), earlier)
        return lax.all_gather(chunk, "z", axis=0).reshape(NZ * tokens, -1)

    g0 = gather((0,))
    g12 = gather((1, 2))

    g0, want = after((g0, want), ())
    out0 = pick(want, g0, 0, 1)
    in0 = exchange(out0)
    g3 = gather((3,), (out0,))
    rows0 = attend(places, queries, [(in0, 0)], 0)
    all0 = spread(rows0)

    (g12,) = after((g12,), all0[1:] + [weights[1], weights[3]])
    out12 = pick(want, g12, 0, 2)
    in12 = exchange(out12)
    g4 = gather((4,), (out12,))
    out3 = pick(want, g3, 0, 1)
    in12, out3 = after((in12, out3), (weights[2],))
    in3 = exchange(out3)
    rows12 = attend(places, queries, [(in12, 0), (in12, 1)], 1)
    all12 = spread(rows12)

    g4, _ = after((g4, rows12), ())
    out4 = pick(want, g4, 0, 1)
    in3, out4 = after((in3, out4), ())
    in4 = exchange(out4)
    rows3 = attend(places, queries, [(in3, 0)], 3)
    all3 = spread(rows3)

    (in4,) = after((in4,), (rows3,))
    rows4 = attend(places, queries, [(in4, 0)], 4)
    all4 = spread(rows4)
    held = after(all0 + all12 + all3, (rows4,))
    terms = [(held[:groups], 0), (held[groups : 2 * groups], 1), (held[2 * groups :], 3)]
    total = project(terms, weights, None, jnp.float32)
    return project([(all4, 4)], weights, total, jnp.bfloat16)


def solution(mesh):
    fine = Mesh(
        mesh.devices.reshape(NY, NZ, NC, mesh.shape["head"]), ("y", "z", "core", "head")
    )
    seq = ("y", "z", "core")
    in_specs = (
        P(seq, "head"),
        P(seq, "head"),
        P(seq, "head"),
        P("head", None),
        P(seq, None),
        P(),
    )
    return jax.shard_map(
        per_device, mesh=fine, in_specs=in_specs, out_specs=P(seq, "head"), check_vma=False
    )
```

```python
import functools

import jax
import jax.numpy as jnp
from jax import lax
from jax.experimental import pallas as pl
from jax.experimental.pallas import tpu as pltpu
from jax.sharding import Mesh
from jax.sharding import PartitionSpec as P

HEAD_DIM = 128
CUBE = 64
SEL = 16
NY, NZ, NC = 4, 8, 2
NPLANE = NY * NC
LOG2_E = 1.4426950408889634


def shift(n, d):
    return [(i, (i + d) % n) for i in range(n)]


def rows_of(at):
    return pl.ds(pl.multiple_of(at * CUBE, CUBE), CUBE)


def pick_kernel(cube_ref, *refs, blocks):
    sources, out = refs[:-1], refs[-1]
    width = 2 * HEAD_DIM
    for head, source in enumerate(sources):
        lanes = pl.ds(head * width, width)

        def step(at, carry, source=source, lanes=lanes):
            out[rows_of(at), lanes] = source[rows_of(cube_ref[at]), :]
            return carry

        lax.fori_loop(0, blocks, step, 0, unroll=8)


def pick(cubes, source, first, heads):
    width = 2 * HEAD_DIM
    rows, blocks = source.shape[0], cubes.shape[0]
    out = jax.ShapeDtypeStruct((blocks * CUBE, heads * width), jnp.bfloat16)
    return pl.pallas_call(
        functools.partial(pick_kernel, blocks=blocks),
        out_shape=out,
        grid_spec=pltpu.PrefetchScalarGridSpec(
            num_scalar_prefetch=1,
            grid=(1,),
            in_specs=[
                pl.BlockSpec((rows, width), lambda i, *_, at=at: (0, at))
                for at in range(first, first + heads)
            ],
            out_specs=pl.BlockSpec(out.shape, lambda i, *_: (0, 0)),
        ),
        cost_estimate=pl.CostEstimate(flops=0, bytes_accessed=4 * out.size, transcendentals=0),
        compiler_params=pltpu.CompilerParams(vmem_limit_bytes=40 << 20),
        name="pick",
    )(cubes, *[source] * heads)


def attend_kernel(place_ref, *refs, cubes, per):
    heads = (len(refs) - 3) // 2
    asking, arrived, (o_ref, ks, vs) = refs[:heads], refs[heads:-3], refs[-3:]
    for head in range(heads):
        lanes = pl.ds(head * HEAD_DIM, HEAD_DIM)

        def step(group, carry, q_ref=asking[head], kv_ref=arrived[head], lanes=lanes):
            for u in range(per):
                for t in range(SEL):
                    rows = rows_of(place_ref[(group * per + u) * SEL + t])
                    ks[u, t * CUBE : (t + 1) * CUBE, :] = kv_ref[rows, :HEAD_DIM]
                    vs[u, t * CUBE : (t + 1) * CUBE, :] = kv_ref[rows, HEAD_DIM:]
            for u in range(per):
                rows = rows_of(group * per + u)
                scores = lax.dot_general(
                    q_ref[rows, :],
                    ks[u],
                    (((1,), (1,)), ((), ())),
                    preferred_element_type=jnp.float32,
                )
                peak = jnp.max(scores, axis=1, keepdims=True)
                raised = jnp.exp2((scores - peak) * (HEAD_DIM**-0.5 * LOG2_E))
                total = jnp.sum(raised, axis=1, keepdims=True)
                probs = (raised * (1.0 / total)).astype(jnp.bfloat16)
                mixed = jnp.dot(probs, vs[u], preferred_element_type=jnp.float32)
                o_ref[rows, lanes] = mixed.astype(jnp.bfloat16)
            return carry

        lax.fori_loop(0, cubes // per, step, 0)


def attend(places, queries, arrived, first):
    tokens, width = queries.shape[0], len(arrived) * HEAD_DIM
    cubes = tokens // CUBE
    per = next(p for p in (4, 3, 2, 1) if cubes % p == 0)
    return pl.pallas_call(
        functools.partial(attend_kernel, cubes=cubes, per=per),
        out_shape=jax.ShapeDtypeStruct((tokens, width), jnp.bfloat16),
        grid_spec=pltpu.PrefetchScalarGridSpec(
            num_scalar_prefetch=1,
            grid=(1,),
            in_specs=[
                pl.BlockSpec((tokens, HEAD_DIM), lambda i, _, head=head: (0, head))
                for head in range(first, first + len(arrived))
            ]
            + [
                pl.BlockSpec((a.shape[0], 2 * HEAD_DIM), lambda i, _, at=at: (0, at))
                for a, at in arrived
            ],
            out_specs=pl.BlockSpec((tokens, width), lambda i, _: (0, 0)),
            scratch_shapes=[pltpu.VMEM((per, SEL * CUBE, HEAD_DIM), jnp.bfloat16)] * 2,
        ),
        cost_estimate=pl.CostEstimate(
            flops=4 * tokens * SEL * CUBE * width,
            bytes_accessed=4 * NPLANE * NZ * CUBE * width,
            transcendentals=tokens * SEL * CUBE * len(arrived),
        ),
        compiler_params=pltpu.CompilerParams(vmem_limit_bytes=24 << 20),
        name="attend",
    )(places, *[queries] * len(arrived), *(a for a, _ in arrived))


def project_kernel(*refs, terms, heads):
    rows, weights, before = refs[:terms], refs[terms : terms + heads], refs[terms + heads : -2]
    out, beside = refs[-2:]

    @pl.when(pl.program_id(0) == 0)
    def _():
        at = 0
        for a in rows:
            beside[:, at : at + a.shape[1]] = a[...]
            at += a.shape[1]

    below = jnp.concatenate([w[...] for w in weights], axis=0)
    total = jnp.dot(beside[...], below, preferred_element_type=jnp.float32)
    for earlier in before:
        total = total + earlier[...]
    out[...] = total.astype(out.dtype)


def project(terms, weights, before, out_type):
    rows = [a for group, _ in terms for a in group]
    tokens, columns = rows[0].shape[0], weights[0].shape[1]
    tile = 256
    block = pl.BlockSpec((tokens, tile), lambda n: (0, n))
    in_specs = [pl.BlockSpec(a.shape, lambda n: (0, 0)) for a in rows]
    below = []
    for group, first in terms:
        for a, w in zip(group, weights):
            for head in range(first, first + a.shape[1] // HEAD_DIM):
                in_specs.append(pl.BlockSpec((HEAD_DIM, tile), lambda n, head=head: (head, n)))
                below.append(w)
    extra = [] if before is None else [before]
    width = sum(a.shape[1] for a in rows)
    return pl.pallas_call(
        functools.partial(project_kernel, terms=len(rows), heads=len(below)),
        out_shape=jax.ShapeDtypeStruct((tokens, columns), out_type),
        grid=(columns // tile,),
        in_specs=in_specs + [block] * len(extra),
        out_specs=block,
        scratch_shapes=[pltpu.VMEM((tokens, width), jnp.bfloat16)],
        cost_estimate=pl.CostEstimate(
            flops=2 * tokens * width * columns,
            bytes_accessed=2 * (tokens * width + width * columns + tokens * columns),
            transcendentals=0,
        ),
        compiler_params=pltpu.CompilerParams(vmem_limit_bytes=40 << 20),
        name="project",
    )(*rows, *below, *extra)


def after(arrays, earlier):
    held = lax.optimization_barrier(tuple(arrays) + tuple(earlier))
    return held[: len(arrays)]


def per_device(queries, keys, values, w_out, selected, home):
    tokens, width = queries.shape
    cubes_here = tokens // CUBE
    heads_here = width // HEAD_DIM
    groups = lax.axis_size("head")
    y, z, core = (lax.axis_index(a) for a in ("y", "z", "core"))
    me = lax.axis_index("head")

    def columns(a, h):
        return a[:, h * HEAD_DIM : (h + 1) * HEAD_DIM]

    def exchange(outgoing):
        return lax.all_to_all(outgoing, ("y", "core"), split_axis=0, concat_axis=0, tiled=True)

    def pack(heads):
        pieces = [columns(a, h) for h in heads for a in (keys, values)]
        return jnp.concatenate(pieces, axis=1)

    catalog = jnp.arange(home.shape[0], dtype=jnp.int32)
    slot_of = jnp.sum(
        jnp.where(selected[:, :, None] == catalog[None, None, :], home[None, None, :], 0), axis=2
    ).reshape(-1)
    owner = slot_of // cubes_here
    places = (owner // (NZ * NC) * NC + owner % NC) * NZ + (z - owner // NC % NZ) % NZ

    plane = lax.all_gather(slot_of, ("y", "core"), axis=0)
    owners = plane // cubes_here
    mine = (owners // (NZ * NC) == y) & (owners % NC == core)
    step = (z - owners // NC % NZ) % NZ
    steps = jnp.arange(NZ, dtype=jnp.int32)[:, None]
    matches = mine[:, None, :] & (step[:, None, :] == steps)
    want = jnp.max(jnp.where(matches, plane[:, None, :] % cubes_here, 0), axis=2)
    from_z = (z - steps[:, 0]) % NZ * cubes_here
    want_ring = (want + steps[:, 0] * cubes_here).reshape(-1)
    want = (want + from_z).reshape(-1)

    w_columns = width_out = w_out.shape[1] // groups
    weights = []
    for d in range(groups):
        part = lax.dynamic_slice_in_dim(w_out, (me + d) % groups * w_columns, width_out, axis=1)
        weights.append(lax.ppermute(part, "head", shift(groups, d)) if d else part)

    def spread(rows):
        return [rows] + [lax.ppermute(rows, "head", shift(groups, d)) for d in range(1, groups)]

    def gather(heads, earlier=()):
        (chunk,) = after((pack(heads),), earlier)
        return lax.all_gather(chunk, "z", axis=0).reshape(NZ * tokens, -1)

    def ring(chunk):
        far = tokens // 2
        ups, downs = [chunk], [chunk]
        for s in range(4):
            up, down = ups[-1], downs[-1]
            if s == 3:
                up, down = up[:far], down[far:]
            ups.append(lax.ppermute(up, "z", shift(NZ, 1)))
            downs.append(lax.ppermute(down, "z", shift(NZ, -1)))
        return jnp.concatenate(ups + downs[:0:-1], axis=0)

    g0 = gather((0,))
    g12 = gather((1, 2))

    g0, want = after((g0, want), ())
    out0 = pick(want, g0, 0, 1)
    in0 = exchange(out0)
    g3 = gather((3,), (out0,))
    g4 = ring(after((pack((4,)),), (out0,))[0])
    rows0 = attend(places, queries, [(in0, 0)], 0)
    all0 = spread(rows0)

    (g4,) = after((g4,), (rows0,))
    in4 = exchange(pick(want_ring, g4, 0, 1))
    (g12,) = after((g12,), all0[1:] + [weights[1], weights[3]])
    out12 = pick(want, g12, 0, 2)
    in4, out12 = after((in4, out12), ())
    in12 = exchange(out12)
    rows4 = attend(places, queries, [(in4, 0)], 4)
    all4 = spread(rows4)

    g3, _ = after((g3, rows4), ())
    out3 = pick(want, g3, 0, 1)
    in12, out3 = after((in12, out3), [weights[2]] + all4[1:])
    in3 = exchange(out3)
    rows12 = attend(places, queries, [(in12, 0), (in12, 1)], 1)
    all12 = spread(rows12)

    (in3,) = after((in3,), (rows12,))
    rows3 = attend(places, queries, [(in3, 0)], 3)
    all3 = spread(rows3)
    held = after(all0 + all12 + all4, (rows3,))
    terms = [(held[:groups], 0), (held[groups : 2 * groups], 1), (held[2 * groups :], 4)]
    total = project(terms, weights, None, jnp.float32)
    return project([(all3, 3)], weights, total, jnp.bfloat16)


def solution(mesh):
    fine = Mesh(
        mesh.devices.reshape(NY, NZ, NC, mesh.shape["head"]), ("y", "z", "core", "head")
    )
    seq = ("y", "z", "core")
    in_specs = (
        P(seq, "head"),
        P(seq, "head"),
        P(seq, "head"),
        P("head", None),
        P(seq, None),
        P(),
    )
    return jax.shard_map(
        per_device, mesh=fine, in_specs=in_specs, out_specs=P(seq, "head"), check_vma=False
    )
```
